32 devices in a mesh: date: 8 (over y, x, core), rng: 4 (over z).
Axes of the slice: x: 2, y: 2, z: 4, core: 2. Of those that a mesh axis runs over, the one named last changes fastest.
Arguments:
- slc_re: bfloat16 [8, 2048, 512], P('date', None, 'rng'), may hold values from -170 to 170
- slc_im: bfloat16 [8, 2048, 512], P('date', None, 'rng'), may hold values from -170 to 170
- ref_date: int32 [1], replicated, may hold values from 0 to 7
- gain: float32 [2048], replicated, may hold values from 0.25 to 2
- bperp: int32 [8], replicated, may hold values from -200 to 199
- tdays: int32 [8], replicated, may hold values from 0 to 1899
- mask: int32 [2048, 512], P(None, 'rng'), may hold values from 0 to 1, as said below
Outputs:
- periodogram: float32 [2048, 512, 256], P('date', 'rng')
The draws below stay inside these ranges and needn't reach their ends.
Inputs may be any that keep to these rules, and one draw needn't show every extreme that they name: `mask`: each aligned block of 256 lines by 128 range columns holds exactly 8192 candidates.
All inputs are finite; a program needn't handle non-finite values.
Results may differ from the reference program's by a relative error of at most 0.0067.
Values may be sent and summed in bfloat16 or wider, within the bound.
A program may use at most 192 MiB of HBM per device.

```python
import math
import jax
import jax.numpy as jnp
from jax import lax

LINES = 2048
RG_DEV = 128
HGRID = 16
VGRID = 16
PHASE_Q = 1024
DATES = 8
RG = 512
LINES_DEV = 256
PS_DEV = 8192


def slc_levels(key):
    date_draw = jax.random.uniform(jax.random.fold_in(key, 3), (DATES, 1, 1), jnp.float32, 0.0, 1.0)
    date_levels = jnp.exp(date_draw * math.log(10.0))
    columns = jnp.arange(RG).astype(jnp.float32) / (RG - 1)
    column_slope = jnp.exp(columns * math.log(3.0))
    rough_draw = jax.random.uniform(jax.random.fold_in(key, 4), (1, 1, RG), jnp.float32, -1.0, 1.0)
    column_rough = jnp.exp(rough_draw * math.log(2.0))
    return date_levels * column_slope[None, None, :] * column_rough


def slc_part(key, fold_value):
    levels = slc_levels(key)
    samples = jax.random.truncated_normal(jax.random.fold_in(key, fold_value), -4.0, 4.0, (DATES, LINES, RG), jnp.float32) * 0.7071
    return (samples * levels).astype(jnp.bfloat16)


def draw_slc_re(key, part):
    return slc_part(key, 1)


def draw_slc_im(key, part):
    return slc_part(key, 2)


def draw_mask(key, part):
    lines_blocks = LINES // LINES_DEV
    range_blocks = RG // RG_DEV
    block_total = lines_blocks * range_blocks
    block_cells = LINES_DEV * RG_DEV
    key_list = jax.random.split(jax.random.fold_in(key, 11), block_total)
    orders = jax.vmap(lambda block_key: jax.random.permutation(block_key, block_cells))(key_list)
    chosen = (orders < PS_DEV).astype(jnp.int32)
    blocked = chosen.reshape(lines_blocks, range_blocks, LINES_DEV, RG_DEV)
    return jnp.transpose(blocked, (0, 2, 1, 3)).reshape(LINES, RG)


def touch_ends(result, own_key, smallest, high):
    extent = result.shape
    place = [jax.random.randint(jax.random.fold_in(own_key, axis), (), 0, extent[axis]) for axis in range(len(extent))]
    result = result.at[tuple(place)].set(smallest)
    longest = extent.index(max(extent))
    place[longest] = (place[longest] + 1) % extent[longest]
    return result.at[tuple(place)].set(high)


def setup_inputs(seed: int = 0) -> dict:
    arg_keys = jax.random.split(jax.random.key(seed), 8)
    return {
        "slc_re": draw_slc_re(jax.random.fold_in(arg_keys[7], 71), 0),
        "slc_im": draw_slc_im(jax.random.fold_in(arg_keys[7], 71), 0),
        "ref_date": jax.random.randint(arg_keys[2], (1,), 0, DATES).astype(jnp.int32),
        "gain": jnp.clip(jnp.exp(jax.random.uniform(arg_keys[3], (LINES,), jnp.float32, math.log(0.25), math.log(2.0))), 0.25, 2.0),
        "bperp": touch_ends(jax.random.randint(arg_keys[4], (DATES,), -200, 200), jax.random.fold_in(arg_keys[4], 1), -200, 199).astype(jnp.int32),
        "tdays": touch_ends(jax.random.randint(arg_keys[5], (DATES,), 0, 1900), jax.random.fold_in(arg_keys[5], 1), 0, 1899).astype(jnp.int32),
        "mask": draw_mask(jax.random.fold_in(arg_keys[7], 71), 0),
    }


def dft_tables(length):
    positions = jnp.arange(length, dtype=jnp.int32)
    products = positions[:, None] * positions[None, :] % length
    angles = products.astype(jnp.float32) * (2.0 * math.pi / length)
    return (jnp.cos(angles).astype(jnp.bfloat16), jnp.sin(angles).astype(jnp.bfloat16))

def phase_tables(bperp, tdays):
    grid_points = jnp.arange(HGRID * VGRID, dtype=jnp.int32)
    height_step = grid_points // VGRID
    speed_step = grid_points % VGRID
    quanta = (bperp[:, None] * height_step[None, :] + tdays[:, None] * speed_step[None, :]) % PHASE_Q
    angles = quanta.astype(jnp.float32) * (2.0 * math.pi / PHASE_Q)
    phase_re = jnp.cos(angles).astype(jnp.bfloat16)
    phase_im = jnp.sin(angles).astype(jnp.bfloat16)
    upper = jnp.concatenate([phase_re, -phase_im], axis=1)
    lower = jnp.concatenate([phase_im, phase_re], axis=1)
    return jnp.concatenate([upper, lower], axis=0)

def coherence_map(piece_re, piece_im, phase_table):
    date_count = piece_re.shape[0]
    grid_size = phase_table.shape[1] // 2
    wide_re = piece_re.astype(jnp.float32)
    wide_im = piece_im.astype(jnp.float32)
    stacked = jnp.concatenate([wide_re, wide_im], axis=0)
    table_wide = lax.optimization_barrier(phase_table).astype(jnp.float32)
    spectra = jnp.einsum('dp,dg->pg', stacked, table_wide)
    peri_re = spectra[:, :grid_size]
    peri_im = spectra[:, grid_size:]
    pixel_power = lax.optimization_barrier(jnp.sum(wide_re * wide_re + wide_im * wide_im, axis=0)) / date_count
    return (peri_re * peri_re + peri_im * peri_im) / (date_count * jnp.maximum(pixel_power, 1.0))[:, None]

def reference(slc_re, slc_im, ref_date, gain, bperp, tdays, mask):
    wide_re = slc_re.astype(jnp.float32)
    wide_im = slc_im.astype(jnp.float32)
    power = lax.optimization_barrier(jnp.sum(wide_re * wide_re + wide_im * wide_im, axis=(1, 2))) / (LINES * RG)
    scales = lax.rsqrt(power + 1e-06)
    ref_index = ref_date[0].astype(jnp.int32)
    ref_scale = lax.dynamic_index_in_dim(scales, ref_index, 0, keepdims=False)
    ref_re = lax.dynamic_index_in_dim(wide_re, ref_index, 0, keepdims=False) * ref_scale
    ref_im = lax.dynamic_index_in_dim(wide_im, ref_index, 0, keepdims=False) * ref_scale
    cos_table, sin_table = dft_tables(LINES)
    cos_wide = lax.optimization_barrier(cos_table).astype(jnp.float32)
    sin_wide = lax.optimization_barrier(sin_table).astype(jnp.float32)
    weights = gain[:, None]

    def filter_date(inputs):
        date_re, date_im, date_scale = inputs
        own_re = date_re.astype(jnp.float32) * date_scale
        own_im = date_im.astype(jnp.float32) * date_scale
        ifg_re = (own_re * ref_re + own_im * ref_im).astype(jnp.bfloat16)
        ifg_im = (own_im * ref_re - own_re * ref_im).astype(jnp.bfloat16)
        pair = lax.optimization_barrier(jnp.stack([ifg_re, ifg_im])).astype(jnp.float32)
        cos_part = jnp.einsum('fl,klc->kfc', cos_wide, pair)
        sin_part = jnp.einsum('fl,klc->kfc', sin_wide, pair)
        spec_re = cos_part[0] + sin_part[1]
        spec_im = cos_part[1] - sin_part[0]
        held = jnp.stack([(spec_re * weights).astype(jnp.bfloat16), (spec_im * weights).astype(jnp.bfloat16)])
        held = lax.optimization_barrier(held).astype(jnp.float32)
        back_cos = jnp.einsum('fl,kfc->klc', cos_wide, held)
        back_sin = jnp.einsum('fl,kfc->klc', sin_wide, held)
        filt_re = ((back_cos[0] - back_sin[1]) * (1.0 / LINES)).astype(jnp.bfloat16)
        filt_im = ((back_sin[0] + back_cos[1]) * (1.0 / LINES)).astype(jnp.bfloat16)
        return (filt_re, filt_im)
    filt_re, filt_im = lax.map(filter_date, (slc_re, slc_im, scales))
    phase_table = phase_tables(bperp, tdays)
    line_block = 16
    block_count = LINES // line_block
    moved_re = jnp.moveaxis(filt_re.reshape(DATES, block_count, line_block * RG), 1, 0)
    moved_im = jnp.moveaxis(filt_im.reshape(DATES, block_count, line_block * RG), 1, 0)

    def pixel_block(pieces):
        piece_re, piece_im = pieces
        return coherence_map(piece_re, piece_im, phase_table)
    mapped = lax.map(pixel_block, (moved_re, moved_im))
    mapped = mapped.reshape(LINES, RG, HGRID * VGRID)
    return mapped * mask.astype(jnp.float32)[:, :, None]
```

```python
import functools
import math

import jax
import jax.numpy as jnp
import ml_dtypes
import numpy as np
from jax import lax
from jax.experimental import pallas as pl
from jax.experimental.pallas import tpu as pltpu
from jax.sharding import PartitionSpec as P

HGRID = 16
VGRID = 16
PHASE_Q = 1024
RADIX = 16
ROWS = 16
MESH = pl.DeviceIdType.MESH
VMEM_BYTES = 56 * 1024 * 1024


def broadcast(shard, axis, root):
    mine = lax.axis_index(axis) == root
    return lax.psum(jnp.where(mine, shard, jnp.zeros_like(shard)), axis)


def dft_blocks(length):
    depth = length // RADIX
    first = np.arange(RADIX)[:, None, None]
    freq = first + RADIX * np.arange(depth)[None, :, None]
    line = np.arange(depth)[None, None, :]
    angle = (freq * line % length) * (2.0 * math.pi / length)
    cos, sin = np.cos(angle), np.sin(angle)
    forward = np.concatenate(
        [np.concatenate([cos, sin], axis=2), np.concatenate([-sin, cos], axis=2)], axis=1
    )
    backward = np.transpose(forward, (0, 2, 1)) / length
    return forward.astype(ml_dtypes.bfloat16), backward.astype(ml_dtypes.bfloat16)


def phase_table(bperp, tdays):
    grid_points = jnp.arange(HGRID * VGRID, dtype=jnp.int32)
    height_step = grid_points // VGRID
    speed_step = grid_points % VGRID
    quanta = (
        bperp[:, None] * height_step[None, :] + tdays[:, None] * speed_step[None, :]
    ) % PHASE_Q
    angles = quanta.astype(jnp.float32) * (2.0 * math.pi / PHASE_Q)
    phase_re = jnp.cos(angles)
    phase_im = jnp.sin(angles)
    upper = jnp.concatenate([phase_re, -phase_im], axis=1)
    lower = jnp.concatenate([phase_im, phase_re], axis=1)
    return jnp.stack([upper, lower], axis=1).reshape(-1, 2 * HGRID * VGRID)


def radix4(a, b, c, d, sign):
    sum_re, sum_im = a[0] + c[0], a[1] + c[1]
    dif_re, dif_im = a[0] - c[0], a[1] - c[1]
    other_re, other_im = b[0] + d[0], b[1] + d[1]
    turn_re, turn_im = b[0] - d[0], b[1] - d[1]
    if sign > 0:
        turn_re, turn_im = -turn_im, turn_re
    else:
        turn_re, turn_im = turn_im, -turn_re
    return (
        (sum_re + other_re, sum_im + other_im),
        (dif_re + turn_re, dif_im + turn_im),
        (sum_re - other_re, sum_im - other_im),
        (dif_re - turn_re, dif_im - turn_im),
    )


def twiddle(value, power, sign):
    power %= 16
    if power == 0:
        return value
    re, im = value
    if power == 4:
        return (-im, re) if sign > 0 else (im, -re)
    if power == 2:
        half = math.sqrt(0.5)
        if sign > 0:
            return ((re - im) * half, (re + im) * half)
        return ((re + im) * half, (im - re) * half)
    if power == 6:
        half = math.sqrt(0.5)
        if sign > 0:
            return ((re + im) * -half, (re - im) * half)
        return ((im - re) * half, (re + im) * -half)
    angle = sign * 2.0 * math.pi * power / 16
    cos, sin = math.cos(angle), math.sin(angle)
    return (re * cos - im * sin, re * sin + im * cos)


def dft16(values, sign):
    inner = [radix4(*[values[4 * n1 + n2] for n1 in range(4)], sign) for n2 in range(4)]
    out = [None] * 16
    for k1 in range(4):
        column = [twiddle(inner[n2][k1], n2 * k1, sign) for n2 in range(4)]
        for k2, value in enumerate(radix4(*column, sign)):
            out[k1 + 4 * k2] = value
    return out


def filter_kernel(
    dates, ranges, re_ref, im_ref, ref_re_ref, ref_im_ref, gain_ref, fwd_ref, inv_ref,
    out_ref, spec, back, filt, sums, peer_sums,
    sum_send, sum_recv, send_sem, recv_sem, own_sem,
):
    date = lax.axis_index("date")
    rng = lax.axis_index("rng")
    lines = re_ref.shape[0]
    depth = lines // RADIX
    lines_dev = lines // dates
    pixels = lines * re_ref.shape[1] * ranges

    barrier = pltpu.get_barrier_semaphore()

    def greet(step, carry):
        other = lax.rem(date + step, dates)
        pl.semaphore_signal(barrier, inc=1, device_id=(other, rng), device_id_type=MESH)
        return carry

    lax.fori_loop(1, dates, greet, 0)
    for step in range(1, ranges):
        other = lax.rem(rng + step, ranges)
        pl.semaphore_signal(barrier, inc=1, device_id=(date, other), device_id_type=MESH)

    for k, (a_ref, b_ref) in enumerate(((re_ref, im_ref), (ref_re_ref, ref_im_ref))):
        def add(i, total, a_ref=a_ref, b_ref=b_ref):
            rows = pl.ds(pl.multiple_of(i * 128, 128), 128)
            a = a_ref[rows, :].astype(jnp.float32)
            b = b_ref[rows, :].astype(jnp.float32)
            return total + jnp.sum((a * a + b * b).reshape(16, 8, 128), axis=0)

        sums[k] = lax.fori_loop(0, lines // 128, add, jnp.zeros((8, 128), jnp.float32))

    pl.semaphore_wait(barrier, dates - 1 + ranges - 1)
    sum_copies = []
    for step in range(1, ranges):
        other = lax.rem(rng + step, ranges)
        copy = pltpu.make_async_remote_copy(
            src_ref=sums, dst_ref=peer_sums.at[step - 1],
            send_sem=sum_send.at[step - 1], recv_sem=sum_recv.at[step - 1],
            device_id=(date, other), device_id_type=MESH,
        )
        copy.start()
        sum_copies.append(copy)
    for copy in sum_copies:
        copy.wait()
    total = sums[...]
    for step in range(1, ranges):
        total = total + peer_sums[step - 1]
    power = jnp.sum(total, axis=(1, 2), keepdims=True) * (1.0 / pixels)
    scale = lax.rsqrt(power + 1e-06)
    own_scale, ref_scale = scale[0], scale[1]

    def forward(q, carry):
        values = []
        for l1 in range(RADIX):
            rows = pl.ds(pl.multiple_of(l1 * depth + q * ROWS, ROWS), ROWS)
            own_re = re_ref[rows, :].astype(jnp.float32) * own_scale
            own_im = im_ref[rows, :].astype(jnp.float32) * own_scale
            ref_re = ref_re_ref[rows, :].astype(jnp.float32) * ref_scale
            ref_im = ref_im_ref[rows, :].astype(jnp.float32) * ref_scale
            ifg_re = (own_re * ref_re + own_im * ref_im).astype(jnp.bfloat16)
            ifg_im = (own_im * ref_re - own_re * ref_im).astype(jnp.bfloat16)
            values.append((ifg_re.astype(jnp.float32), ifg_im.astype(jnp.float32)))
        for f1, (re, im) in enumerate(dft16(values, -1)):
            spec[f1, pl.ds(pl.multiple_of(q * ROWS, ROWS), ROWS), :] = re.astype(jnp.bfloat16)
            spec[f1, pl.ds(pl.multiple_of(depth + q * ROWS, ROWS), ROWS), :] = im.astype(
                jnp.bfloat16
            )
        return carry

    lax.fori_loop(0, depth // ROWS, forward, 0)

    def band(f1, carry):
        spectrum = jnp.dot(fwd_ref[f1], spec[f1], preferred_element_type=jnp.float32)
        weight = gain_ref[f1]
        weighted = jnp.concatenate([spectrum[:depth] * weight, spectrum[depth:] * weight], axis=0)
        back[f1] = jnp.dot(
            inv_ref[f1], weighted.astype(jnp.bfloat16), preferred_element_type=jnp.float32
        )
        return carry

    lax.fori_loop(0, RADIX, band, 0, unroll=4)

    def inverse(q, carry):
        top = pl.ds(pl.multiple_of(q * ROWS, ROWS), ROWS)
        low = pl.ds(pl.multiple_of(depth + q * ROWS, ROWS), ROWS)
        values = [(back[f1, top, :], back[f1, low, :]) for f1 in range(RADIX)]
        for l1, (re, im) in enumerate(dft16(values, 1)):
            rows = pl.ds(pl.multiple_of(l1 * depth + q * ROWS, ROWS), ROWS)
            filt[0, rows, :] = re.astype(jnp.bfloat16)
            filt[1, rows, :] = im.astype(jnp.bfloat16)
        return carry

    lax.fori_loop(0, depth // ROWS, inverse, 0)

    def block(owner):
        return filt.at[:, pl.ds(pl.multiple_of(owner * lines_dev, ROWS), lines_dev), :]

    def piece(step):
        other = lax.rem(date + step, dates)
        return pltpu.make_async_remote_copy(
            src_ref=block(other), dst_ref=out_ref.at[date],
            send_sem=send_sem.at[step - 1], recv_sem=recv_sem.at[step - 1],
            device_id=(other, rng), device_id_type=MESH,
        )

    def send(step, carry):
        piece(step).start()
        return carry

    def finish(step, carry):
        piece(step).wait()
        return carry

    own = pltpu.make_async_copy(block(date), out_ref.at[date], own_sem)
    lax.fori_loop(1, dates, send, 0)
    own.start()
    own.wait()
    lax.fori_loop(1, dates, finish, 0)


def filtered_pieces(dates, ranges, re, im, ref_re, ref_im, gain):
    lines, columns = re.shape
    depth = lines // RADIX
    lines_dev = lines // dates
    fwd, inv = dft_blocks(lines)
    weights = jnp.broadcast_to(gain.reshape(depth, RADIX).T[:, :, None], (RADIX, depth, columns))
    vmem = pl.BlockSpec(memory_space=pltpu.VMEM)
    return pl.pallas_call(
        functools.partial(filter_kernel, dates, ranges),
        out_shape=jax.ShapeDtypeStruct((dates, 2, lines_dev, columns), jnp.bfloat16),
        in_specs=[vmem] * 7,
        out_specs=pl.BlockSpec(memory_space=pl.ANY),
        scratch_shapes=[
            pltpu.VMEM((RADIX, 2 * depth, columns), jnp.bfloat16),
            pltpu.VMEM((RADIX, 2 * depth, columns), jnp.float32),
            pltpu.VMEM((2, lines, columns), jnp.bfloat16),
            pltpu.VMEM((2, 8, columns), jnp.float32),
            pltpu.VMEM((ranges - 1, 2, 8, columns), jnp.float32),
            pltpu.SemaphoreType.DMA((ranges - 1,)),
            pltpu.SemaphoreType.DMA((ranges - 1,)),
            pltpu.SemaphoreType.DMA((dates - 1,)),
            pltpu.SemaphoreType.DMA((dates - 1,)),
            pltpu.SemaphoreType.DMA,
        ],
        compiler_params=pltpu.CompilerParams(
            collective_id=0, has_side_effects=True, vmem_limit_bytes=VMEM_BYTES
        ),
        name="filter_exchange",
    )(re, im, ref_re, ref_im, weights, jnp.asarray(fwd), jnp.asarray(inv))


def map_kernel(index_ref, pieces_ref, mask_ref, table_ref, out_ref, turned):
    j = pl.program_id(0)
    dates, _, lines_dev, columns = pieces_ref.shape
    groups = lines_dev // ROWS
    depth = 2 * dates * ROWS
    points = out_ref.shape[-1]

    @pl.when(j == 0)
    def _():
        def turn(g, carry):
            rows = pl.ds(pl.multiple_of(g * ROWS, ROWS), ROWS)
            block = pieces_ref[:, :, rows, :].astype(jnp.float32)
            block = block.reshape(2 * dates, ROWS, columns)
            power = jnp.sum(block * block, axis=0) * (1.0 / dates)
            wanted = mask_ref[rows, :].astype(jnp.float32)
            scale = jnp.sqrt(wanted / (dates * jnp.maximum(power, 1.0)))
            scaled = (block * scale[None]).reshape(depth, columns)
            cols = pl.ds(pl.multiple_of(g * columns, columns), columns)
            turned[cols, :] = scaled.T.astype(jnp.bfloat16)
            return carry

        lax.fori_loop(0, groups, turn, 0)

    row = lax.broadcasted_iota(jnp.int32, (depth, 2 * points), 0)
    table = jnp.where(lax.rem(row, ROWS) == j, table_ref[...], 0.0).astype(jnp.bfloat16)
    batch = min(4, groups)

    def multiply(b, carry):
        rows = pl.ds(pl.multiple_of(b * batch * columns, batch * columns), batch * columns)
        peri = jnp.dot(turned[rows, :], table, preferred_element_type=jnp.float32)
        result = peri[:, :points] * peri[:, :points] + peri[:, points:] * peri[:, points:]
        out_ref[pl.ds(b * batch, batch), 0] = result.reshape(batch, columns, points)
        return carry

    lax.fori_loop(0, groups // batch, multiply, 0)


def coherence_map(pieces, mask, table, index):
    dates, _, lines_dev, columns = pieces.shape
    points = table.shape[1] // 2
    groups = lines_dev // ROWS
    depth = 2 * dates * ROWS
    tall = jnp.repeat(table.astype(jnp.bfloat16).astype(jnp.float32), ROWS, axis=0)
    mapped = pl.pallas_call(
        map_kernel,
        out_shape=jax.ShapeDtypeStruct((groups, ROWS, columns, points), jnp.float32),
        grid_spec=pltpu.PrefetchScalarGridSpec(
            num_scalar_prefetch=1,
            grid=(ROWS,),
            in_specs=[
                pl.BlockSpec((dates, 2, lines_dev, columns), lambda j, index: (0, 0, 0, 0)),
                pl.BlockSpec((lines_dev, columns), lambda j, index: (index[0], 0)),
                pl.BlockSpec((depth, 2 * points), lambda j, index: (0, 0)),
            ],
            out_specs=pl.BlockSpec((groups, 1, columns, points), lambda j, index: (0, j, 0, 0)),
            scratch_shapes=[pltpu.VMEM((groups * columns, depth), jnp.bfloat16)],
        ),
        compiler_params=pltpu.CompilerParams(vmem_limit_bytes=VMEM_BYTES),
        name="coherence_map",
    )(index, pieces, mask, tall)
    return mapped.reshape(lines_dev, columns, points)


def shards(slc_re, slc_im, ref_date, gain, bperp, tdays, mask):
    dates = lax.axis_size("date")
    ranges = lax.axis_size("rng")
    own_re, own_im = slc_re[0], slc_im[0]
    ref_re, ref_im = (
        broadcast(own_re, "date", ref_date[0]),
        broadcast(own_im, "date", ref_date[0]),
    )
    pieces = filtered_pieces(dates, ranges, own_re, own_im, ref_re, ref_im, gain)
    index = lax.axis_index("date").astype(jnp.int32).reshape(1)
    return coherence_map(pieces, mask, phase_table(bperp, tdays), index)


def solution(mesh):
    in_specs = (P("date", None, "rng"), P("date", None, "rng"), P(), P(), P(), P(), P(None, "rng"))
    out_specs = P("date", "rng", None)
    return jax.shard_map(shards, mesh=mesh, in_specs=in_specs, out_specs=out_specs, check_vma=False)
```

```python
import functools
import math

import jax
import jax.numpy as jnp
import ml_dtypes
import numpy as np
from jax import lax
from jax.experimental import pallas as pl
from jax.experimental.pallas import tpu as pltpu
from jax.sharding import PartitionSpec as P

HGRID = 16
VGRID = 16
PHASE_Q = 1024
RADIX = 16
CHUNKS = 8
ROWS = 16
MESH = pl.DeviceIdType.MESH
VMEM_BYTES = 56 * 1024 * 1024


def broadcast(shard, axis, root):
    mine = lax.axis_index(axis) == root
    return lax.psum(jnp.where(mine, shard, jnp.zeros_like(shard)), axis)


def dft_blocks(length):
    depth = length // RADIX
    first = np.arange(RADIX)[:, None, None]
    freq = first + RADIX * np.arange(depth)[None, :, None]
    line = np.arange(depth)[None, None, :]
    angle = (freq * line % length) * (2.0 * math.pi / length)
    cos, sin = np.cos(angle), np.sin(angle)
    forward = np.concatenate(
        [np.concatenate([cos, sin], axis=2), np.concatenate([-sin, cos], axis=2)], axis=1
    )
    backward = np.transpose(forward, (0, 2, 1)) / length
    return forward.astype(ml_dtypes.bfloat16), backward.astype(ml_dtypes.bfloat16)


def phase_table(bperp, tdays):
    grid_points = jnp.arange(HGRID * VGRID, dtype=jnp.int32)
    height_step = grid_points // VGRID
    speed_step = grid_points % VGRID
    quanta = (
        bperp[:, None] * height_step[None, :] + tdays[:, None] * speed_step[None, :]
    ) % PHASE_Q
    angles = quanta.astype(jnp.float32) * (2.0 * math.pi / PHASE_Q)
    phase_re = jnp.cos(angles)
    phase_im = jnp.sin(angles)
    upper = jnp.concatenate([phase_re, -phase_im], axis=1)
    lower = jnp.concatenate([phase_im, phase_re], axis=1)
    return jnp.stack([upper, lower], axis=1).reshape(-1, 2 * HGRID * VGRID)


def radix4(a, b, c, d, sign):
    sum_re, sum_im = a[0] + c[0], a[1] + c[1]
    dif_re, dif_im = a[0] - c[0], a[1] - c[1]
    other_re, other_im = b[0] + d[0], b[1] + d[1]
    turn_re, turn_im = b[0] - d[0], b[1] - d[1]
    if sign > 0:
        turn_re, turn_im = -turn_im, turn_re
    else:
        turn_re, turn_im = turn_im, -turn_re
    return (
        (sum_re + other_re, sum_im + other_im),
        (dif_re + turn_re, dif_im + turn_im),
        (sum_re - other_re, sum_im - other_im),
        (dif_re - turn_re, dif_im - turn_im),
    )


def twiddle(value, power, sign):
    power %= 16
    if power == 0:
        return value
    re, im = value
    if power == 4:
        return (-im, re) if sign > 0 else (im, -re)
    if power == 2:
        half = math.sqrt(0.5)
        if sign > 0:
            return ((re - im) * half, (re + im) * half)
        return ((re + im) * half, (im - re) * half)
    if power == 6:
        half = math.sqrt(0.5)
        if sign > 0:
            return ((re + im) * -half, (re - im) * half)
        return ((im - re) * half, (re + im) * -half)
    angle = sign * 2.0 * math.pi * power / 16
    cos, sin = math.cos(angle), math.sin(angle)
    return (re * cos - im * sin, re * sin + im * cos)


def dft16(values, sign):
    inner = [radix4(*[values[4 * n1 + n2] for n1 in range(4)], sign) for n2 in range(4)]
    out = [None] * 16
    for k1 in range(4):
        column = [twiddle(inner[n2][k1], n2 * k1, sign) for n2 in range(4)]
        for k2, value in enumerate(radix4(*column, sign)):
            out[k1 + 4 * k2] = value
    return out


def local_power(re_ref, im_ref):
    def add(i, total):
        rows = pl.ds(pl.multiple_of(i * 128, 128), 128)
        a = re_ref[rows, :].astype(jnp.float32)
        b = im_ref[rows, :].astype(jnp.float32)
        return total + jnp.sum((a * a + b * b).reshape(16, 8, 128), axis=0)

    return lax.fori_loop(0, re_ref.shape[0] // 128, add, jnp.zeros((8, 128), jnp.float32))


def share_kernel(
    owner, dates, ranges, re_ref, im_ref, image_ref, total_ref, sums, peer_sums,
    sum_send, sum_recv, total_send, total_recv, send_sem, recv_sem, own_sem,
):
    date = lax.axis_index("date")
    rng = lax.axis_index("rng")
    inputs = (re_ref, im_ref)
    chunk = re_ref.shape[0] // CHUNKS
    barrier = pltpu.get_barrier_semaphore()
    for step in range(1, dates):
        other = lax.rem(date + step, dates)
        pl.semaphore_signal(barrier, inc=1, device_id=(other, rng), device_id_type=MESH)
    for step in range(1, ranges):
        other = lax.rem(rng + step, ranges)
        pl.semaphore_signal(barrier, inc=1, device_id=(date, other), device_id_type=MESH)
    sums[...] = local_power(re_ref, im_ref)
    pl.semaphore_wait(barrier, dates - 1 + ranges - 1)

    def sum_copy(step):
        return pltpu.make_async_remote_copy(
            src_ref=sums, dst_ref=peer_sums.at[step - 1],
            send_sem=sum_send.at[step - 1], recv_sem=sum_recv.at[step - 1],
            device_id=(date, lax.rem(rng + step, ranges)), device_id_type=MESH,
        )

    def finish_sums():
        total = sums[...]
        for step in range(1, ranges):
            sum_copy(step).wait()
            total = total + peer_sums[step - 1]
        total_ref[0] = total

    def total_copy(step):
        return pltpu.make_async_remote_copy(
            src_ref=total_ref.at[0], dst_ref=total_ref.at[1],
            send_sem=total_send.at[step - 1], recv_sem=total_recv,
            device_id=((owner + step) % dates, rng), device_id_type=MESH,
        )

    def image_copy(k, n, way, target):
        rows = pl.ds(n * chunk, chunk)
        return lambda source: pltpu.make_async_remote_copy(
            src_ref=source.at[rows, :], dst_ref=image_ref.at[k, rows, :],
            send_sem=send_sem.at[k, n, way], recv_sem=recv_sem.at[k, n],
            device_id=(target, rng), device_id_type=MESH,
        )

    for step in range(1, ranges):
        sum_copy(step).start()

    o, o2 = owner, owner ^ 1
    x, x2 = owner ^ 2, owner ^ 3
    y, y2 = owner ^ 4, owner ^ 5
    z, z2 = owner ^ 6, owner ^ 7

    @pl.when(date == o)
    def _():
        def copies(n):
            made = []
            for k in range(2):
                for way, target in enumerate(((x, y)[k], o2)):
                    made.append(image_copy(k, n, way, target)(inputs[k]))
            return made

        ahead = 3
        for n in range(ahead):
            for copy in copies(n):
                copy.start()
        finish_sums()
        for step in range(1, dates):
            total_copy(step).start()
        total_ref[1] = total_ref[0]
        for n in range(ahead, CHUNKS + ahead):
            for copy in copies(n - ahead):
                copy.wait_send()
            if n < CHUNKS:
                for copy in copies(n):
                    copy.start()
        for k in range(2):
            own = pltpu.make_async_copy(inputs[k], image_ref.at[k], own_sem.at[k])
            own.start()
            own.wait()
        for step in range(1, dates):
            total_copy(step).wait_send()

    routes = (
        (x, x2, (z, None), (1, 3)),
        (y, y2, (None, z), (3, 1)),
        (z, z2, (y, x), (2, 2)),
    )
    for device, partner, onward, delays in routes:
        @pl.when(date == device)
        def _(device=device, partner=partner, onward=onward, delays=delays):
            started = []
            for t in range(CHUNKS + 3):
                for k in range(2):
                    n = t - delays[k]
                    if not 0 <= n < CHUNKS:
                        continue
                    image_copy(k, n, 1, partner)(image_ref.at[k]).wait_recv()
                    for way, target in enumerate((onward[k], partner)):
                        if target is not None:
                            copy = image_copy(k, n, way, target)(image_ref.at[k])
                            copy.start()
                            started.append(copy)
            finish_sums()
            for copy in started:
                copy.wait_send()
            total_copy(1).wait_recv()

    for device in (o2, x2, y2, z2):
        @pl.when(date == device)
        def _(device=device):
            finish_sums()
            for n in range(CHUNKS):
                for k in range(2):
                    image_copy(k, n, 1, device ^ 1)(image_ref.at[k]).wait_recv()
            total_copy(1).wait_recv()


def share_from(owner, dates, ranges, re, im):
    lines, columns = re.shape
    vmem = pl.BlockSpec(memory_space=pltpu.VMEM)
    return pl.pallas_call(
        functools.partial(share_kernel, owner, dates, ranges),
        out_shape=(
            jax.ShapeDtypeStruct((2, lines, columns), jnp.bfloat16),
            jax.ShapeDtypeStruct((2, 8, columns), jnp.float32),
        ),
        in_specs=[vmem] * 2,
        out_specs=(vmem, vmem),
        scratch_shapes=[
            pltpu.VMEM((8, columns), jnp.float32),
            pltpu.VMEM((ranges - 1, 8, columns), jnp.float32),
            pltpu.SemaphoreType.DMA((ranges - 1,)),
            pltpu.SemaphoreType.DMA((ranges - 1,)),
            pltpu.SemaphoreType.DMA((dates - 1,)),
            pltpu.SemaphoreType.DMA,
            pltpu.SemaphoreType.DMA((2, CHUNKS, 2)),
            pltpu.SemaphoreType.DMA((2, CHUNKS)),
            pltpu.SemaphoreType.DMA((2,)),
        ],
        compiler_params=pltpu.CompilerParams(
            collective_id=1 + owner, has_side_effects=True, vmem_limit_bytes=VMEM_BYTES
        ),
        name=f"share_{owner}",
    )(re, im)


def power_rows(re, im):
    wide_re, wide_im = re.astype(jnp.float32), im.astype(jnp.float32)
    return jnp.sum((wide_re * wide_re + wide_im * wide_im).reshape(-1, 8, re.shape[1]), axis=0)


def share_reference(dates, ranges, re, im, ref_date):
    if dates == 8:
        branches = [functools.partial(share_from, owner, dates, ranges) for owner in range(dates)]
        return lax.switch(ref_date, branches, re, im)
    image = jnp.stack([broadcast(re, "date", ref_date), broadcast(im, "date", ref_date)])
    sums = jnp.stack([power_rows(re, im), power_rows(image[0], image[1])])
    return image, lax.psum(sums, "rng")


def filter_kernel(
    dates, ranges, re_ref, im_ref, image_ref, total_ref, gain_ref, fwd_ref, inv_ref,
    out_ref, spec, back, filt, send_sem, recv_sem, own_sem,
):
    date = lax.axis_index("date")
    rng = lax.axis_index("rng")
    lines = re_ref.shape[0]
    depth = lines // RADIX
    lines_dev = lines // dates
    pixels = lines * re_ref.shape[1] * ranges

    barrier = pltpu.get_barrier_semaphore()

    def greet(step, carry):
        other = lax.rem(date + step, dates)
        pl.semaphore_signal(barrier, inc=1, device_id=(other, rng), device_id_type=MESH)
        return carry

    lax.fori_loop(1, dates, greet, 0)
    power = jnp.sum(total_ref[...], axis=(1, 2), keepdims=True) * (1.0 / pixels)
    scale = lax.rsqrt(power + 1e-06)
    own_scale, ref_scale = scale[0], scale[1]

    def forward(q, carry):
        values = []
        for l1 in range(RADIX):
            rows = pl.ds(pl.multiple_of(l1 * depth + q * ROWS, ROWS), ROWS)
            own_re = re_ref[rows, :].astype(jnp.float32) * own_scale
            own_im = im_ref[rows, :].astype(jnp.float32) * own_scale
            ref_re = image_ref[0, rows, :].astype(jnp.float32) * ref_scale
            ref_im = image_ref[1, rows, :].astype(jnp.float32) * ref_scale
            ifg_re = (own_re * ref_re + own_im * ref_im).astype(jnp.bfloat16)
            ifg_im = (own_im * ref_re - own_re * ref_im).astype(jnp.bfloat16)
            values.append((ifg_re.astype(jnp.float32), ifg_im.astype(jnp.float32)))
        for f1, (re, im) in enumerate(dft16(values, -1)):
            spec[f1, pl.ds(pl.multiple_of(q * ROWS, ROWS), ROWS), :] = re.astype(jnp.bfloat16)
            spec[f1, pl.ds(pl.multiple_of(depth + q * ROWS, ROWS), ROWS), :] = im.astype(
                jnp.bfloat16
            )
        return carry

    lax.fori_loop(0, depth // ROWS, forward, 0)

    def band(f1, carry):
        spectrum = jnp.dot(fwd_ref[f1], spec[f1], preferred_element_type=jnp.float32)
        weight = gain_ref[f1]
        weighted = jnp.concatenate([spectrum[:depth] * weight, spectrum[depth:] * weight], axis=0)
        back[f1] = jnp.dot(
            inv_ref[f1], weighted.astype(jnp.bfloat16), preferred_element_type=jnp.float32
        )
        return carry

    lax.fori_loop(0, RADIX, band, 0, unroll=4)

    def inverse(q, carry):
        top = pl.ds(pl.multiple_of(q * ROWS, ROWS), ROWS)
        low = pl.ds(pl.multiple_of(depth + q * ROWS, ROWS), ROWS)
        values = [(back[f1, top, :], back[f1, low, :]) for f1 in range(RADIX)]
        for l1, (re, im) in enumerate(dft16(values, 1)):
            rows = pl.ds(pl.multiple_of(l1 * depth + q * ROWS, ROWS), ROWS)
            filt[0, rows, :] = re.astype(jnp.bfloat16)
            filt[1, rows, :] = im.astype(jnp.bfloat16)
        return carry

    lax.fori_loop(0, depth // ROWS, inverse, 0)

    def block(owner):
        return filt.at[:, pl.ds(pl.multiple_of(owner * lines_dev, ROWS), lines_dev), :]

    def piece(step):
        other = lax.rem(date + step, dates)
        return pltpu.make_async_remote_copy(
            src_ref=block(other), dst_ref=out_ref.at[date],
            send_sem=send_sem.at[step - 1], recv_sem=recv_sem.at[step - 1],
            device_id=(other, rng), device_id_type=MESH,
        )

    def send(step, carry):
        piece(step).start()
        return carry

    def finish(step, carry):
        piece(step).wait()
        return carry

    pl.semaphore_wait(barrier, dates - 1)
    own = pltpu.make_async_copy(block(date), out_ref.at[date], own_sem)
    lax.fori_loop(1, dates, send, 0)
    own.start()
    own.wait()
    lax.fori_loop(1, dates, finish, 0)


def filtered_pieces(dates, ranges, re, im, image, totals, gain):
    lines, columns = re.shape
    depth = lines // RADIX
    lines_dev = lines // dates
    fwd, inv = dft_blocks(lines)
    weights = jnp.broadcast_to(gain.reshape(depth, RADIX).T[:, :, None], (RADIX, depth, columns))
    vmem = pl.BlockSpec(memory_space=pltpu.VMEM)
    return pl.pallas_call(
        functools.partial(filter_kernel, dates, ranges),
        out_shape=jax.ShapeDtypeStruct((dates, 2, lines_dev, columns), jnp.bfloat16),
        in_specs=[vmem] * 7,
        out_specs=pl.BlockSpec(memory_space=pl.ANY),
        scratch_shapes=[
            pltpu.VMEM((RADIX, 2 * depth, columns), jnp.bfloat16),
            pltpu.VMEM((RADIX, 2 * depth, columns), jnp.float32),
            pltpu.VMEM((2, lines, columns), jnp.bfloat16),
            pltpu.SemaphoreType.DMA((dates - 1,)),
            pltpu.SemaphoreType.DMA((dates - 1,)),
            pltpu.SemaphoreType.DMA,
        ],
        compiler_params=pltpu.CompilerParams(
            collective_id=0, has_side_effects=True, vmem_limit_bytes=VMEM_BYTES
        ),
        name="filter_exchange",
    )(re, im, image, totals, weights, jnp.asarray(fwd), jnp.asarray(inv))


def map_kernel(index_ref, pieces_ref, mask_ref, table_ref, out_ref, turned):
    j = pl.program_id(0)
    dates, _, lines_dev, columns = pieces_ref.shape
    groups = lines_dev // ROWS
    depth = 2 * dates * ROWS
    points = out_ref.shape[-1]

    @pl.when(j == 0)
    def _():
        def turn(g, carry):
            rows = pl.ds(pl.multiple_of(g * ROWS, ROWS), ROWS)
            block = pieces_ref[:, :, rows, :].astype(jnp.float32)
            block = block.reshape(2 * dates, ROWS, columns)
            power = jnp.sum(block * block, axis=0) * (1.0 / dates)
            wanted = mask_ref[rows, :].astype(jnp.float32)
            scale = jnp.sqrt(wanted / (dates * jnp.maximum(power, 1.0)))
            scaled = (block * scale[None]).reshape(depth, columns)
            cols = pl.ds(pl.multiple_of(g * columns, columns), columns)
            turned[cols, :] = scaled.T.astype(jnp.bfloat16)
            return carry

        lax.fori_loop(0, groups, turn, 0)

    row = lax.broadcasted_iota(jnp.int32, (depth, 2 * points), 0)
    table = jnp.where((row & (ROWS - 1)) == j, table_ref[...], 0.0).astype(jnp.bfloat16)
    batch = min(4, groups)

    def multiply(b, carry):
        rows = pl.ds(pl.multiple_of(b * batch * columns, batch * columns), batch * columns)
        peri = jnp.dot(turned[rows, :], table, preferred_element_type=jnp.float32)
        result = peri[:, :points] * peri[:, :points] + peri[:, points:] * peri[:, points:]
        out_ref[pl.ds(b * batch, batch), 0] = result.reshape(batch, columns, points)
        return carry

    lax.fori_loop(0, groups // batch, multiply, 0, unroll=True)


def coherence_map(pieces, mask, table, index):
    dates, _, lines_dev, columns = pieces.shape
    points = table.shape[1] // 2
    groups = lines_dev // ROWS
    depth = 2 * dates * ROWS
    tall = jnp.repeat(table.astype(jnp.bfloat16).astype(jnp.float32), ROWS, axis=0)
    mapped = pl.pallas_call(
        map_kernel,
        out_shape=jax.ShapeDtypeStruct((groups, ROWS, columns, points), jnp.float32),
        grid_spec=pltpu.PrefetchScalarGridSpec(
            num_scalar_prefetch=1,
            grid=(ROWS,),
            in_specs=[
                pl.BlockSpec((dates, 2, lines_dev, columns), lambda j, index: (0, 0, 0, 0)),
                pl.BlockSpec((lines_dev, columns), lambda j, index: (index[0], 0)),
                pl.BlockSpec((depth, 2 * points), lambda j, index: (0, 0)),
            ],
            out_specs=pl.BlockSpec((groups, 1, columns, points), lambda j, index: (0, j, 0, 0)),
            scratch_shapes=[pltpu.VMEM((groups * columns, depth), jnp.bfloat16)],
        ),
        compiler_params=pltpu.CompilerParams(vmem_limit_bytes=VMEM_BYTES),
        name="coherence_map",
    )(index, pieces, mask, tall)
    return mapped.reshape(lines_dev, columns, points)


def shards(slc_re, slc_im, ref_date, gain, bperp, tdays, mask):
    dates = lax.axis_size("date")
    ranges = lax.axis_size("rng")
    own_re, own_im = slc_re[0], slc_im[0]
    image, totals = share_reference(dates, ranges, own_re, own_im, ref_date[0])
    pieces = filtered_pieces(dates, ranges, own_re, own_im, image, totals, gain)
    index = lax.axis_index("date").astype(jnp.int32).reshape(1)
    return coherence_map(pieces, mask, phase_table(bperp, tdays), index)


def solution(mesh):
    in_specs = (P("date", None, "rng"), P("date", None, "rng"), P(), P(), P(), P(), P(None, "rng"))
    out_specs = P("date", "rng", None)
    return jax.shard_map(shards, mesh=mesh, in_specs=in_specs, out_specs=out_specs, check_vma=False)
```

```python
import functools
import math

import jax
import jax.numpy as jnp
import ml_dtypes
import numpy as np
from jax import lax
from jax.experimental import pallas as pl
from jax.experimental.pallas import tpu as pltpu
from jax.sharding import PartitionSpec as P

HGRID = 16
VGRID = 16
PHASE_Q = 1024
RADIX = 16
CHUNKS = 8
ROWS = 16
MESH = pl.DeviceIdType.MESH
VMEM_BYTES = 56 * 1024 * 1024


def broadcast(shard, axis, root):
    mine = lax.axis_index(axis) == root
    return lax.psum(jnp.where(mine, shard, jnp.zeros_like(shard)), axis)


def dft_blocks(length):
    depth = length // RADIX
    first = np.arange(RADIX)[:, None, None]
    freq = first + RADIX * np.arange(depth)[None, :, None]
    line = np.arange(depth)[None, None, :]
    angle = (freq * line % length) * (2.0 * math.pi / length)
    cos, sin = np.cos(angle), np.sin(angle)
    forward = np.concatenate(
        [np.concatenate([cos, sin], axis=2), np.concatenate([-sin, cos], axis=2)], axis=1
    )
    backward = np.transpose(forward, (0, 2, 1)) / length
    return forward.astype(ml_dtypes.bfloat16), backward.astype(ml_dtypes.bfloat16)


def phase_table(bperp, tdays):
    grid_points = jnp.arange(HGRID * VGRID, dtype=jnp.int32)
    height_step = grid_points // VGRID
    speed_step = grid_points % VGRID
    quanta = (
        bperp[:, None] * height_step[None, :] + tdays[:, None] * speed_step[None, :]
    ) % PHASE_Q
    angles = quanta.astype(jnp.float32) * (2.0 * math.pi / PHASE_Q)
    phase_re = jnp.cos(angles)
    phase_im = jnp.sin(angles)
    half = HGRID * VGRID // 2
    upper, lower = [], []
    for part in (slice(0, half), slice(half, 2 * half)):
        upper += [phase_re[:, part], -phase_im[:, part]]
        lower += [phase_im[:, part], phase_re[:, part]]
    rows = [jnp.concatenate(upper, axis=1), jnp.concatenate(lower, axis=1)]
    return jnp.concatenate(rows, axis=0).astype(jnp.bfloat16).astype(jnp.float32)


def radix4(a, b, c, d, sign):
    sum_re, sum_im = a[0] + c[0], a[1] + c[1]
    dif_re, dif_im = a[0] - c[0], a[1] - c[1]
    other_re, other_im = b[0] + d[0], b[1] + d[1]
    turn_re, turn_im = b[0] - d[0], b[1] - d[1]
    if sign > 0:
        turn_re, turn_im = -turn_im, turn_re
    else:
        turn_re, turn_im = turn_im, -turn_re
    return (
        (sum_re + other_re, sum_im + other_im),
        (dif_re + turn_re, dif_im + turn_im),
        (sum_re - other_re, sum_im - other_im),
        (dif_re - turn_re, dif_im - turn_im),
    )


def twiddle(value, power, sign):
    power %= 16
    if power == 0:
        return value
    re, im = value
    if power == 4:
        return (-im, re) if sign > 0 else (im, -re)
    if power == 2:
        half = math.sqrt(0.5)
        if sign > 0:
            return ((re - im) * half, (re + im) * half)
        return ((re + im) * half, (im - re) * half)
    if power == 6:
        half = math.sqrt(0.5)
        if sign > 0:
            return ((re + im) * -half, (re - im) * half)
        return ((im - re) * half, (re + im) * -half)
    angle = sign * 2.0 * math.pi * power / 16
    cos, sin = math.cos(angle), math.sin(angle)
    return (re * cos - im * sin, re * sin + im * cos)


def dft16(values, sign):
    inner = [radix4(*[values[4 * n1 + n2] for n1 in range(4)], sign) for n2 in range(4)]
    out = [None] * 16
    for k1 in range(4):
        column = [twiddle(inner[n2][k1], n2 * k1, sign) for n2 in range(4)]
        for k2, value in enumerate(radix4(*column, sign)):
            out[k1 + 4 * k2] = value
    return out


def local_power(re_ref, im_ref):
    def add(i, total):
        rows = pl.ds(pl.multiple_of(i * 128, 128), 128)
        a = re_ref[rows, :].astype(jnp.float32)
        b = im_ref[rows, :].astype(jnp.float32)
        return total + jnp.sum((a * a + b * b).reshape(16, 8, 128), axis=0)

    return lax.fori_loop(0, re_ref.shape[0] // 128, add, jnp.zeros((8, 128), jnp.float32))


def share_kernel(
    owner, dates, ranges, re_ref, im_ref, image_ref, total_ref, sums, peer_sums,
    sum_send, sum_recv, total_send, total_recv, send_sem, recv_sem, own_sem,
):
    date = lax.axis_index("date")
    rng = lax.axis_index("rng")
    inputs = (re_ref, im_ref)
    chunk = re_ref.shape[0] // CHUNKS
    barrier = pltpu.get_barrier_semaphore()
    for step in range(1, dates):
        other = lax.rem(date + step, dates)
        pl.semaphore_signal(barrier, inc=1, device_id=(other, rng), device_id_type=MESH)
    for step in range(1, ranges):
        other = lax.rem(rng + step, ranges)
        pl.semaphore_signal(barrier, inc=1, device_id=(date, other), device_id_type=MESH)
    sums[...] = local_power(re_ref, im_ref)
    pl.semaphore_wait(barrier, dates - 1 + ranges - 1)

    def sum_copy(step):
        return pltpu.make_async_remote_copy(
            src_ref=sums, dst_ref=peer_sums.at[step - 1],
            send_sem=sum_send.at[step - 1], recv_sem=sum_recv.at[step - 1],
            device_id=(date, lax.rem(rng + step, ranges)), device_id_type=MESH,
        )

    def finish_sums():
        total = sums[...]
        for step in range(1, ranges):
            sum_copy(step).wait()
            total = total + peer_sums[step - 1]
        total_ref[0] = total

    def total_copy(step):
        return pltpu.make_async_remote_copy(
            src_ref=total_ref.at[0], dst_ref=total_ref.at[1],
            send_sem=total_send.at[step - 1], recv_sem=total_recv,
            device_id=((owner + step) % dates, rng), device_id_type=MESH,
        )

    def image_copy(k, n, way, target):
        rows = pl.ds(n * chunk, chunk)
        return lambda source: pltpu.make_async_remote_copy(
            src_ref=source.at[rows, :], dst_ref=image_ref.at[k, rows, :],
            send_sem=send_sem.at[k, n, way], recv_sem=recv_sem.at[k, n],
            device_id=(target, rng), device_id_type=MESH,
        )

    for step in range(1, ranges):
        sum_copy(step).start()

    o, o2 = owner, owner ^ 1
    x, x2 = owner ^ 2, owner ^ 3
    y, y2 = owner ^ 4, owner ^ 5
    z, z2 = owner ^ 6, owner ^ 7

    @pl.when(date == o)
    def _():
        def copies(n):
            made = []
            for k in range(2):
                for way, target in enumerate(((x, y)[k], o2)):
                    made.append(image_copy(k, n, way, target)(inputs[k]))
            return made

        owns = [
            pltpu.make_async_copy(inputs[k], image_ref.at[k], own_sem.at[k]) for k in range(2)
        ]
        ahead = 4
        for n in range(ahead):
            for copy in copies(n):
                copy.start()
        for own in owns:
            own.start()
        finish_sums()
        for step in range(1, dates):
            total_copy(step).start()
        total_ref[1] = total_ref[0]
        for n in range(ahead, CHUNKS + ahead):
            for copy in copies(n - ahead):
                copy.wait_send()
            if n < CHUNKS:
                for copy in copies(n):
                    copy.start()
        for own in owns:
            own.wait()
        for step in range(1, dates):
            total_copy(step).wait_send()

    routes = (
        (x, x2, (z, None), (0, 6)),
        (y, y2, (None, z), (6, 0)),
        (z, z2, (y, x), (0, 0)),
    )
    for device, partner, onward, delays in routes:
        @pl.when(date == device)
        def _(device=device, partner=partner, onward=onward, delays=delays):
            started = []
            for t in range(CHUNKS + 6):
                for k in range(2):
                    n = t - delays[k]
                    if not 0 <= n < CHUNKS:
                        continue
                    image_copy(k, n, 1, partner)(image_ref.at[k]).wait_recv()
                    for way, target in enumerate((onward[k], partner)):
                        if target is not None:
                            copy = image_copy(k, n, way, target)(image_ref.at[k])
                            copy.start()
                            started.append(copy)
            finish_sums()
            for copy in started:
                copy.wait_send()
            total_copy(1).wait_recv()

    for device in (o2, x2, y2, z2):
        @pl.when(date == device)
        def _(device=device):
            finish_sums()
            for n in range(CHUNKS):
                for k in range(2):
                    image_copy(k, n, 1, device ^ 1)(image_ref.at[k]).wait_recv()
            total_copy(1).wait_recv()


def share_from(owner, dates, ranges, re, im):
    lines, columns = re.shape
    vmem = pl.BlockSpec(memory_space=pltpu.VMEM)
    return pl.pallas_call(
        functools.partial(share_kernel, owner, dates, ranges),
        out_shape=(
            jax.ShapeDtypeStruct((2, lines, columns), jnp.bfloat16),
            jax.ShapeDtypeStruct((2, 8, columns), jnp.float32),
        ),
        in_specs=[vmem] * 2,
        out_specs=(vmem, vmem),
        scratch_shapes=[
            pltpu.VMEM((8, columns), jnp.float32),
            pltpu.VMEM((ranges - 1, 8, columns), jnp.float32),
            pltpu.SemaphoreType.DMA((ranges - 1,)),
            pltpu.SemaphoreType.DMA((ranges - 1,)),
            pltpu.SemaphoreType.DMA((dates - 1,)),
            pltpu.SemaphoreType.DMA,
            pltpu.SemaphoreType.DMA((2, CHUNKS, 2)),
            pltpu.SemaphoreType.DMA((2, CHUNKS)),
            pltpu.SemaphoreType.DMA((2,)),
        ],
        compiler_params=pltpu.CompilerParams(
            collective_id=1 + owner, has_side_effects=True, vmem_limit_bytes=VMEM_BYTES
        ),
        name=f"share_{owner}",
    )(re, im)


def power_rows(re, im):
    wide_re, wide_im = re.astype(jnp.float32), im.astype(jnp.float32)
    return jnp.sum((wide_re * wide_re + wide_im * wide_im).reshape(-1, 8, re.shape[1]), axis=0)


def share_reference(dates, ranges, re, im, ref_date):
    if dates == 8:
        branches = [functools.partial(share_from, owner, dates, ranges) for owner in range(dates)]
        return lax.switch(ref_date, branches, re, im)
    image = jnp.stack([broadcast(re, "date", ref_date), broadcast(im, "date", ref_date)])
    sums = jnp.stack([power_rows(re, im), power_rows(image[0], image[1])])
    return image, lax.psum(sums, "rng")


def filter_kernel(
    dates, ranges, re_ref, im_ref, image_ref, total_ref, gain_ref, fwd_ref, inv_ref,
    out_ref, spec, back, filt, fwd, inv, send_sem, recv_sem, own_sem, table_sem,
):
    date = lax.axis_index("date")
    rng = lax.axis_index("rng")
    lines = re_ref.shape[0]
    depth = lines // RADIX
    lines_dev = lines // dates
    pixels = lines * re_ref.shape[1] * ranges

    loads = [
        pltpu.make_async_copy(fwd_ref, fwd, table_sem.at[0]),
        pltpu.make_async_copy(inv_ref, inv, table_sem.at[1]),
    ]
    for load in loads:
        load.start()
    barrier = pltpu.get_barrier_semaphore()

    def greet(step, carry):
        other = lax.rem(date + step, dates)
        pl.semaphore_signal(barrier, inc=1, device_id=(other, rng), device_id_type=MESH)
        return carry

    lax.fori_loop(1, dates, greet, 0)
    power = jnp.sum(total_ref[...], axis=(1, 2), keepdims=True) * (1.0 / pixels)
    scale = lax.rsqrt(power + 1e-06)
    own_scale, ref_scale = scale[0], scale[1]

    def forward(q, carry):
        values = []
        for l1 in range(RADIX):
            rows = pl.ds(pl.multiple_of(l1 * depth + q * ROWS, ROWS), ROWS)
            own_re = re_ref[rows, :].astype(jnp.float32) * own_scale
            own_im = im_ref[rows, :].astype(jnp.float32) * own_scale
            ref_re = image_ref[0, rows, :].astype(jnp.float32) * ref_scale
            ref_im = image_ref[1, rows, :].astype(jnp.float32) * ref_scale
            ifg_re = (own_re * ref_re + own_im * ref_im).astype(jnp.bfloat16)
            ifg_im = (own_im * ref_re - own_re * ref_im).astype(jnp.bfloat16)
            values.append((ifg_re.astype(jnp.float32), ifg_im.astype(jnp.float32)))
        for f1, (re, im) in enumerate(dft16(values, -1)):
            spec[f1, pl.ds(pl.multiple_of(q * ROWS, ROWS), ROWS), :] = re.astype(jnp.bfloat16)
            spec[f1, pl.ds(pl.multiple_of(depth + q * ROWS, ROWS), ROWS), :] = im.astype(
                jnp.bfloat16
            )
        return carry

    lax.fori_loop(0, depth // ROWS, forward, 0)

    for load in loads:
        load.wait()

    def band(f1, carry):
        spectrum = jnp.dot(fwd[f1], spec[f1], preferred_element_type=jnp.float32)
        weight = jnp.broadcast_to(gain_ref[pl.ds(f1, 1), :], (spectrum.shape[1], depth)).T
        weighted = jnp.concatenate([spectrum[:depth] * weight, spectrum[depth:] * weight], axis=0)
        back[f1] = jnp.dot(
            inv[f1], weighted.astype(jnp.bfloat16), preferred_element_type=jnp.float32
        )
        return carry

    lax.fori_loop(0, RADIX, band, 0, unroll=4)

    def inverse(q, carry):
        top = pl.ds(pl.multiple_of(q * ROWS, ROWS), ROWS)
        low = pl.ds(pl.multiple_of(depth + q * ROWS, ROWS), ROWS)
        values = [(back[f1, top, :], back[f1, low, :]) for f1 in range(RADIX)]
        for l1, (re, im) in enumerate(dft16(values, 1)):
            rows = pl.ds(pl.multiple_of(l1 * depth + q * ROWS, ROWS), ROWS)
            filt[0, rows, :] = re.astype(jnp.bfloat16)
            filt[1, rows, :] = im.astype(jnp.bfloat16)
        return carry

    lax.fori_loop(0, depth // ROWS, inverse, 0)

    def block(owner):
        return filt.at[:, pl.ds(pl.multiple_of(owner * lines_dev, ROWS), lines_dev), :]

    def piece(step):
        other = lax.rem(date + step, dates)
        return pltpu.make_async_remote_copy(
            src_ref=block(other), dst_ref=out_ref.at[:, date],
            send_sem=send_sem.at[step - 1], recv_sem=recv_sem.at[step - 1],
            device_id=(other, rng), device_id_type=MESH,
        )

    def send(step, carry):
        piece(step).start()
        return carry

    def finish(step, carry):
        piece(step).wait()
        return carry

    pl.semaphore_wait(barrier, dates - 1)
    own = pltpu.make_async_copy(block(date), out_ref.at[:, date], own_sem)
    lax.fori_loop(1, dates, send, 0)
    own.start()
    own.wait()
    lax.fori_loop(1, dates, finish, 0)


def filtered_pieces(dates, ranges, re, im, image, totals, gain):
    lines, columns = re.shape
    depth = lines // RADIX
    lines_dev = lines // dates
    fwd, inv = dft_blocks(lines)
    weights = gain.reshape(depth, RADIX).T
    vmem = pl.BlockSpec(memory_space=pltpu.VMEM)
    return pl.pallas_call(
        functools.partial(filter_kernel, dates, ranges),
        out_shape=jax.ShapeDtypeStruct((2, dates, lines_dev, columns), jnp.bfloat16),
        in_specs=[vmem] * 5 + [pl.BlockSpec(memory_space=pl.ANY)] * 2,
        out_specs=pl.BlockSpec(memory_space=pl.ANY),
        scratch_shapes=[
            pltpu.VMEM((RADIX, 2 * depth, columns), jnp.bfloat16),
            pltpu.VMEM((RADIX, 2 * depth, columns), jnp.float32),
            pltpu.VMEM((2, lines, columns), jnp.bfloat16),
            pltpu.VMEM(fwd.shape, jnp.bfloat16),
            pltpu.VMEM(inv.shape, jnp.bfloat16),
            pltpu.SemaphoreType.DMA((dates - 1,)),
            pltpu.SemaphoreType.DMA((dates - 1,)),
            pltpu.SemaphoreType.DMA,
            pltpu.SemaphoreType.DMA((2,)),
        ],
        compiler_params=pltpu.CompilerParams(
            collective_id=0, has_side_effects=True, vmem_limit_bytes=VMEM_BYTES
        ),
        name="filter_exchange",
    )(re, im, image, totals, weights, jnp.asarray(fwd), jnp.asarray(inv))


def map_kernel(index_ref, pieces_ref, mask_ref, table_ref, out_ref, turned, tall):
    j = pl.program_id(0)
    _, dates, lines_dev, columns = pieces_ref.shape
    groups = lines_dev // ROWS
    depth = 2 * dates * ROWS
    points = out_ref.shape[-1]

    @pl.when(j == 0)
    def _():
        def turn(g, carry):
            rows = pl.ds(pl.multiple_of(g * ROWS, ROWS), ROWS)
            block = pieces_ref[:, :, rows, :].astype(jnp.float32)
            block = block.reshape(2 * dates, ROWS, columns)
            power = jnp.sum(block * block, axis=0) * (1.0 / dates)
            wanted = mask_ref[rows, :].astype(jnp.float32)
            scale = jnp.sqrt(wanted / (dates * jnp.maximum(power, 1.0)))
            scaled = (block * scale[None]).reshape(depth, columns)
            cols = pl.ds(pl.multiple_of(g * columns, columns), columns)
            turned[cols, :] = scaled.T.astype(jnp.bfloat16)
            return carry

        lax.fori_loop(0, groups, turn, 0, unroll=2)
        for k in range(2 * dates):
            tall[pl.ds(k * ROWS, ROWS), :] = jnp.broadcast_to(
                table_ref[pl.ds(k, 1), :], (ROWS, 2 * points)
            )

    row = lax.broadcasted_iota(jnp.int32, (depth, 2 * points), 0)
    table = jnp.where((row & (ROWS - 1)) == j, tall[...], 0.0).astype(jnp.bfloat16)
    batch = min(4, groups)

    def multiply(b, carry):
        rows = pl.ds(pl.multiple_of(b * batch * columns, batch * columns), batch * columns)
        source = turned[rows, :]
        half = points // 2
        for part in range(2):
            peri = jnp.dot(
                source, table[:, part * points:(part + 1) * points],
                preferred_element_type=jnp.float32,
            )
            result = peri[:, :half] * peri[:, :half] + peri[:, half:] * peri[:, half:]
            out_ref[pl.ds(b * batch, batch), 0, :, pl.ds(part * half, half)] = result.reshape(
                batch, columns, half
            )
        return carry

    lax.fori_loop(0, groups // batch, multiply, 0, unroll=True)


def coherence_map(pieces, mask, table, index):
    _, dates, lines_dev, columns = pieces.shape
    points = table.shape[1] // 2
    groups = lines_dev // ROWS
    depth = 2 * dates * ROWS
    mapped = pl.pallas_call(
        map_kernel,
        out_shape=jax.ShapeDtypeStruct((groups, ROWS, columns, points), jnp.float32),
        grid_spec=pltpu.PrefetchScalarGridSpec(
            num_scalar_prefetch=1,
            grid=(ROWS,),
            in_specs=[
                pl.BlockSpec((2, dates, lines_dev, columns), lambda j, index: (0, 0, 0, 0)),
                pl.BlockSpec((lines_dev, columns), lambda j, index: (index[0], 0)),
                pl.BlockSpec((2 * dates, 2 * points), lambda j, index: (0, 0)),
            ],
            out_specs=pl.BlockSpec((groups, 1, columns, points), lambda j, index: (0, j, 0, 0)),
            scratch_shapes=[
                pltpu.VMEM((groups * columns, depth), jnp.bfloat16),
                pltpu.VMEM((depth, 2 * points), jnp.float32),
            ],
        ),
        compiler_params=pltpu.CompilerParams(vmem_limit_bytes=VMEM_BYTES),
        name="coherence_map",
    )(index, pieces, mask, table)
    return mapped.reshape(lines_dev, columns, points)


def shards(slc_re, slc_im, ref_date, gain, bperp, tdays, mask):
    dates = lax.axis_size("date")
    ranges = lax.axis_size("rng")
    own_re, own_im = slc_re[0], slc_im[0]
    image, totals = share_reference(dates, ranges, own_re, own_im, ref_date[0])
    pieces = filtered_pieces(dates, ranges, own_re, own_im, image, totals, gain)
    index = lax.axis_index("date").astype(jnp.int32).reshape(1)
    return coherence_map(pieces, mask, phase_table(bperp, tdays), index)


def solution(mesh):
    in_specs = (P("date", None, "rng"), P("date", None, "rng"), P(), P(), P(), P(), P(None, "rng"))
    out_specs = P("date", "rng", None)
    return jax.shard_map(shards, mesh=mesh, in_specs=in_specs, out_specs=out_specs, check_vma=False)
```
